32 devices in a mesh: clips: 2 (over x), rows: 16 (over z, y, core).
Axes of the slice: x: 2, y: 2, z: 4, core: 2. Of those that a mesh axis runs over, the one named last changes fastest.
Arguments:
- state_start: bfloat16 [1024, 128, 128], P(('clips', 'rows')), parts along dimension 0, may hold values from -6 to 6
- features: bfloat16 [2, 1024, 128, 128], P(None, ('clips', 'rows')), parts along dimension 1, may hold values from -6 to 6
- row_moves: int32 [2, 2048], P(None, ('clips', 'rows')), parts along dimension 1, may hold values from -4 to 4, as said below
- col_moves: int32 [2, 2048], P(None, ('clips', 'rows')), parts along dimension 1, may hold values from -4 to 4
- merging_weight: bfloat16 [3, 3, 256, 128], replicated, may hold values from -0.125 to 0.125
- first_weight: bfloat16 [3, 3, 128, 128], replicated, may hold values from -0.1875 to 0.1875
- second_weight: bfloat16 [3, 3, 128, 128], replicated, may hold values from -0.1875 to 0.1875
Outputs:
- states: bfloat16 [2, 1024, 128, 128], P(None, ('clips', 'rows')), parts along dimension 1
The draws below stay inside these ranges and needn't reach their ends.
There are 2 independent parts, one for each index of `clips`. The reference program is written for one: setup_inputs(seed, part) draws one part's arguments, and reference() takes and returns one part's arrays. A program takes and returns all parts, laid end to end along the dimension named above; an argument that names none is the same for every part. Nothing has to cross between parts.
Inputs may be any that keep to these rules, and one draw needn't show every extreme that they name: `row_moves`: every source block lies on the destination block's own device or on the device just above or below it; in each frame, among the 64 destination blocks of one device at most 32 take their source from the device above and at most 32 from the device below, and some device takes exactly 32 from the device above and some device exactly 32 from the one below.
All inputs are finite; a program needn't handle non-finite values.
Results may differ from the reference program's by a relative error of at most 0.009.
Values may be sent and summed in bfloat16 or wider, within the bound.
A program may use at most 64 MiB of HBM per device.

```python
import jax
import jax.numpy as jnp

C = 128
FRAMES = 2
MOVE = 4
ROWS_DEV = 32
W = 128
H = 512
BLOCKS = 1024
N_ROWS = 16


def draw_row_moves(key, part):
    band = ROWS_DEV // 8
    across = W // 8
    key_speed, key_sign, key_force, key_cols, key_jitter = jax.random.split(key, 5)
    level = jax.random.randint(key_speed, (FRAMES, N_ROWS), 0, 8)
    speed = jnp.where(level < 2, MOVE, level % 2)
    sign = jnp.where(jax.random.randint(key_sign, (FRAMES, N_ROWS), 0, 2) == 0, -1, 1)
    forced = jax.random.randint(key_force, (FRAMES, 1), 1, N_ROWS - 2)
    device = jnp.arange(N_ROWS)[None, :]
    speed = jnp.where((device == forced) | (device == forced + 1), MOVE, speed)
    sign = jnp.where(device == forced, -1, jnp.where(device == forced + 1, 1, sign))
    col_keys = jax.random.split(key_cols, FRAMES * N_ROWS)
    ranking = jax.vmap(lambda one_key: jax.random.permutation(one_key, across))(col_keys)
    ranking = ranking.reshape(FRAMES, N_ROWS, 1, across)
    moving = ranking < across // 2
    row_in = jnp.arange(band)[None, None, :, None]
    jitter = jax.random.randint(key_jitter, (FRAMES, N_ROWS, band, across), -1, 2)
    still = jnp.clip(row_in + jitter, 0, band - 1) - row_in
    fast = (sign * speed)[:, :, None, None]
    moves = jnp.where(moving, fast, still)
    return moves.reshape(FRAMES, BLOCKS).astype(jnp.int32)


def touch_ends(drawn, own_key, low, high):
    longest = drawn.shape.index(max(drawn.shape))
    spots = []
    for shift in (0, 1):
        where = [jax.random.randint(jax.random.fold_in(own_key, axis), (), 0, length) for axis, length in enumerate(drawn.shape)]
        where[longest] = (where[longest] + shift) % drawn.shape[longest]
        spots.append(tuple(where))
    return drawn.at[spots[0]].set(low).at[spots[1]].set(high)


def block_levels(key, extent, cuts, low, largest):
    def one(dim, shards_of):
        draws = jax.random.uniform(jax.random.fold_in(jax.random.fold_in(key, 6), dim), (shards_of,), jnp.float32, low / len(cuts), largest / len(cuts))
        return jnp.repeat(jnp.exp(draws), extent[dim] // shards_of).reshape((-1,) + (1,) * (len(extent) - dim - 1))

    loudness = one(*cuts[0])
    for cut in cuts[1:]:
        loudness = loudness * one(*cut)
    return loudness


def bell_draw(own_key, dims, deviation, limit, cuts=(), kind=jnp.bfloat16):
    result = deviation * jax.random.normal(own_key, dims, jnp.float32)
    if cuts:
        result = result * block_levels(own_key, dims, cuts, -0.22, 0.18)
    return jnp.clip(result, -limit, limit).astype(kind)


def setup_inputs(seed: int = 0, part: int = 0) -> dict:
    arg_keys = jax.random.split(jax.random.key(seed), 8)
    part_splits = jax.random.split(jax.random.fold_in(arg_keys[7], part), 8)
    return {
        "state_start": bell_draw(part_splits[0], (H, W, C), 1.0, 6.0, ((0, 16),)),
        "features": bell_draw(part_splits[1], (FRAMES, H, W, C), 1.0, 6.0, ((1, 16),)),
        "row_moves": draw_row_moves(jax.random.fold_in(jax.random.fold_in(arg_keys[7], part), 71), part),
        "col_moves": touch_ends(jax.random.randint(part_splits[3], (FRAMES, BLOCKS), -4, 5), jax.random.fold_in(part_splits[3], 1), -4, 4).astype(jnp.int32),
        "merging_weight": bell_draw(arg_keys[4], (3, 3, 2 * C, C), (9 * 2 * C) ** -0.5, 0.125),
        "first_weight": bell_draw(arg_keys[5], (3, 3, C, C), (9 * C) ** -0.5, 0.1875),
        "second_weight": bell_draw(arg_keys[6], (3, 3, C, C), (9 * C) ** -0.5, 0.1875),
    }


def convolve(padded, weight):
    out_rows = padded.shape[0] - 2
    col_count = padded.shape[1]
    in_chan = padded.shape[2]
    widened = jnp.pad(padded, ((0, 0), (1, 1), (0, 0)))
    shifted = jnp.concatenate([widened[:, 0:col_count], widened[:, 1:col_count + 1], widened[:, 2:col_count + 2]], axis=-1)
    summed = jnp.zeros((out_rows * col_count, weight.shape[3]), jnp.float32)
    for row_step in range(3):
        window = shifted[row_step:row_step + out_rows].reshape(out_rows * col_count, 3 * in_chan)
        taps = weight[row_step].reshape(3 * in_chan, weight.shape[3])
        summed = summed + jnp.dot(window, taps, preferred_element_type=jnp.float32)
    return summed.reshape(out_rows, col_count, weight.shape[3])


def pad_rows(field):
    return jnp.pad(field, ((1, 1), (0, 0), (0, 0)))


def fetch(previous, moves_down, moves_across):
    row_count, col_count, chan_count = previous.shape
    band_total = row_count // 8
    across = col_count // 8
    block_ids = jnp.arange(band_total * across).astype(jnp.int32)
    source_row = jnp.clip(block_ids // across + moves_down, 0, band_total - 1).astype(jnp.int32)
    source_col = jnp.clip(block_ids % across + moves_across, 0, across - 1).astype(jnp.int32)
    blocked = previous.reshape(band_total, 8, across, 8, chan_count)
    picked = blocked[source_row, :, source_col]
    picked = picked.reshape(band_total, across, 8, 8, chan_count)
    return picked.transpose(0, 2, 1, 3, 4).reshape(row_count, col_count, chan_count)


def reference(state_start, features, row_moves, col_moves, merging_weight, first_weight, second_weight):
    previous = state_start
    results = []
    for frame in range(FRAMES):
        warped = fetch(previous, row_moves[frame], col_moves[frame])
        joined = jnp.concatenate([features[frame], warped], axis=-1)
        raw = convolve(pad_rows(joined), merging_weight)
        merging = jnp.maximum(raw, 0.1 * raw).astype(jnp.bfloat16)
        middle = jnp.maximum(convolve(pad_rows(merging), first_weight), 0.0).astype(jnp.bfloat16)
        updated = (merging.astype(jnp.float32) + convolve(pad_rows(middle), second_weight)).astype(jnp.bfloat16)
        results.append(updated)
        previous = updated
    return jnp.stack(results)
```

```python
import functools

import jax
import jax.numpy as jnp
from jax import lax
from jax.experimental import pallas as pl
from jax.experimental.pallas import tpu as pltpu
from jax.sharding import PartitionSpec as P

BLOCK = 8
MESH = pl.DeviceIdType.MESH
F32 = jnp.float32
BF16 = jnp.bfloat16


def put_taps(dst, row, values, rows):
    cols, chan = dst.shape[1], dst.shape[2] // 3
    length = rows * cols
    col = lax.rem(lax.broadcasted_iota(jnp.int32, (length, chan), 0), cols)
    left = jnp.where(col == 0, 0.0, pltpu.roll(values, 1, 0))
    right = jnp.where(col == cols - 1, 0.0, pltpu.roll(values, length - 1, 0))
    for e, part in enumerate((left, values, right)):
        dst[pl.ds(row, rows), :, e * chan : (e + 1) * chan] = part.astype(BF16).reshape(rows, cols, chan)


def conv_pairs(src, pair, count, weight):
    cols, depth = src.shape[1], src.shape[2]
    rows = src[pl.ds(2 * pair, 2 * count + 2)].reshape(count + 1, 2, cols, depth)
    window = jnp.concatenate([rows[:count, 0], rows[:count, 1], rows[1:, 0], rows[1:, 1]], axis=-1)
    return jnp.dot(window.reshape(count * cols, 4 * depth), weight[...], preferred_element_type=F32)


def unpair(values, count, cols):
    chan = values.shape[1] // 2
    even = values[:, :chan].reshape(count, cols, chan)
    odd = values[:, chan:].reshape(count, cols, chan)
    return jnp.stack([even, odd], axis=1).reshape(2 * count * cols, chan)


def kernel(
    group, picks, lists, state, features, w_merge, w_first, w_second, out,
    st, ft, wm, w1, w2, own, pool, packed, xf, xw, xm, xd, acc, wp, ob,
    big_f, big_w, big_1, big_2, want_v, want, halo_f, halo_w,
    load_sem, want_sem, out_sem, send_sem, recv_sem,
):
    frames, rows, cols, chan = features.shape
    band, across = rows // BLOCK, cols // BLOCK
    blocks = band * across
    slots = blocks // 2
    area = BLOCK * BLOCK
    me = lax.axis_index("rows")
    has = (me > 0, me < group - 1)
    peer = (me - 1, me + 1)

    loads = [
        pltpu.make_async_copy(a, b, load_sem.at[i])
        for i, (a, b) in enumerate(((state, st), (features, ft), (w_merge, wm), (w_first, w1), (w_second, w2)))
    ]
    for load in loads:
        load.start()

    barrier = pltpu.get_barrier_semaphore()
    for side in (0, 1):
        @pl.when(has[side])
        def _():
            pl.semaphore_signal(barrier, inc=1, device_id={"rows": peer[side]}, device_id_type=MESH)
    pl.semaphore_wait(barrier, has[0].astype(jnp.int32) + has[1].astype(jnp.int32))

    def remote(kind, side, src, dst):
        return pltpu.make_async_remote_copy(
            src_ref=src, dst_ref=dst,
            send_sem=send_sem.at[kind, side], recv_sem=recv_sem.at[kind, 1 - side],
            device_id={"rows": peer[side]}, device_id_type=MESH,
        )

    def list_copy(side):
        return remote(0, side, lists.at[side], want_v.at[1 - side])

    def feature_copy(side):
        edge = pl.ds(0, 3) if side == 0 else pl.ds(rows - 3, 3)
        return remote(1, side, features.at[:, edge], halo_f.at[1 - side])

    def pack_copy(f, side):
        return remote(2 + f, side, packed.at[f, side], pool[f].at[pl.ds(blocks + (1 - side) * slots, slots)])

    def halo_copy(f, side):
        edge = pl.ds(0, 3) if side == 0 else pl.ds(rows - 3, 3)
        return remote(2 + frames + f, side, wp.at[f, edge], halo_w.at[f, 1 - side])

    def each_side(action):
        for side in (0, 1):
            @pl.when(has[side])
            def _():
                action(side)

    def arrived(copy_of, side):
        copy_of(1 - side).wait_recv()

    each_side(lambda side: list_copy(side).start())
    each_side(lambda side: feature_copy(side).start())

    def to_blocks(f, b, q, strip):
        for h in (0, 1):
            block = strip[:, h * BLOCK : (h + 1) * BLOCK].reshape(area, chan).astype(BF16)
            own[f][b * across + 2 * q + h] = block
            pool[f][b * across + 2 * q + h] = block

    loads[0].wait()

    def cut_body(i, carry):
        b, q = i // (across // 2), i % (across // 2)
        strip = st[pl.ds(b * BLOCK, BLOCK), pl.ds(pl.multiple_of(q * 2 * BLOCK, 2 * BLOCK), 2 * BLOCK), :]
        to_blocks(0, b, q, strip.astype(F32))
        return carry

    lax.fori_loop(0, blocks // 2, cut_body, 0)

    for side in (0, 1):
        @pl.when(has[side])
        def _():
            arrived(list_copy, side)
            fetch = pltpu.make_async_copy(want_v.at[side], want.at[side], want_sem.at[side])
            fetch.start()
            fetch.wait()

    def pack_and_send(f):
        def action(side):
            def body(k, carry):
                for u in range(4):
                    packed[f, side, 4 * k + u] = own[f][want[side, f, 4 * k + u]]
                return carry
            lax.fori_loop(0, slots // 4, body, 0)
            pack_copy(f, side).start()
        each_side(action)

    pack_and_send(0)

    for load in loads[2:]:
        load.wait()

    def widen(big, raw, first):
        for t in range(4):
            for e in range(3):
                spot = pl.ds((t * 3 + e) * chan, chan)
                for r in (0, 1):
                    lanes = slice(r * chan, (r + 1) * chan)
                    if 0 <= t - r <= 2:
                        big[spot, lanes] = raw[t - r, e, first : first + chan, :]
                    else:
                        big[spot, lanes] = jnp.zeros((chan, chan), BF16)

    widen(big_f, wm, 0)
    widen(big_w, wm, chan)
    widen(big_1, w1, 0)
    widen(big_2, w2, 0)

    loads[1].wait()

    def fill_taps(dst, src, offset, total, step):
        def body(i, carry):
            values = src[pl.ds(i * step, step)].astype(F32).reshape(step * cols, chan)
            put_taps(dst, offset + i * step, values, step)
            return carry
        lax.fori_loop(0, total // step, body, 0)

    def edge_rows(dst, buffer, side):
        start = 0 if side == 0 else rows + 3
        values = buffer[...].astype(F32).reshape(3 * cols, chan)
        put_taps(dst, start, values, 3)

    def edge_zero(dst, start, count):
        dst[pl.ds(start, count)] = jnp.zeros((count,) + dst.shape[1:], BF16)

    for f in range(frames):
        fill_taps(xf.at[f], ft.at[f], 3, rows, 4)
    for side in (0, 1):
        @pl.when(has[side])
        def _():
            arrived(feature_copy, side)
            for f in range(frames):
                edge_rows(xf.at[f], halo_f.at[side, f], side)

        @pl.when(jnp.logical_not(has[side]))
        def _():
            for f in range(frames):
                edge_zero(xf.at[f], 0 if side == 0 else rows + 3, 3)
            edge_zero(xw, 0 if side == 0 else rows + 3, 3)

    pairs = rows // 2
    for f in range(frames):
        def feature_body(i, carry):
            count = (pairs + 2) // 3
            acc[f, pl.ds(i * count, count)] = conv_pairs(xf.at[f], i * count, count, big_f).reshape(count, cols, 2 * chan)
            return carry
        lax.fori_loop(0, 3, feature_body, 0)

    def merge_pairs(f, pair, count):
        total = acc[f, pl.ds(pair, count)].reshape(count * cols, 2 * chan) + conv_pairs(xw, pair, count, big_w)
        total = jnp.maximum(total, 0.1 * total)
        put_taps(xm, 2 * pair, unpair(total, count, cols), 2 * count)

    for f in range(frames):
        each_side(lambda side: arrived(functools.partial(pack_copy, f), side))

        def gather_body(i, carry):
            b, q = i // (across // 2), i % (across // 2)
            halves = [
                pool[f][picks[f, b * across + 2 * q + h]].astype(F32).reshape(BLOCK, BLOCK, chan) for h in (0, 1)
            ]
            strip = jnp.concatenate(halves, axis=1).astype(BF16)
            wp[f, pl.ds(b * BLOCK, BLOCK), pl.ds(pl.multiple_of(q * 2 * BLOCK, 2 * BLOCK), 2 * BLOCK), :] = strip
            return carry

        half = across // 2
        lax.fori_loop(0, half, gather_body, 0)
        lax.fori_loop((band - 1) * half, band * half, gather_body, 0)
        each_side(lambda side: halo_copy(f, side).start())
        lax.fori_loop(half, (band - 1) * half, gather_body, 0)
        fill_taps(xw, wp.at[f], 3, rows, 4)

        inner = (pairs - 2) // 2
        lax.fori_loop(0, 2, lambda i, c: (merge_pairs(f, 2 + i * inner, inner), c)[1], 0)
        for side in (0, 1):
            @pl.when(has[side])
            def _():
                arrived(functools.partial(halo_copy, f), side)
                edge_rows(xw, halo_w.at[f, side], side)
            merge_pairs(f, 0 if side == 0 else pairs, 2)

            @pl.when(jnp.logical_not(has[side]))
            def _():
                edge_zero(xm, 0 if side == 0 else rows + 2, 2)

        count = (pairs + 1 + 2) // 3

        def middle_body(i, carry):
            pair = jnp.minimum(i * count, pairs + 1 - count)
            total = jnp.maximum(conv_pairs(xm, pair, count, big_1), 0.0)
            put_taps(xd, 2 * pair, unpair(total, count, cols), 2 * count)
            return carry

        lax.fori_loop(0, 3, middle_body, 0)
        for side in (0, 1):
            @pl.when(jnp.logical_not(has[side]))
            def _():
                edge_zero(xd, 0 if side == 0 else rows + 1, 1)

        per = BLOCK // 2

        def last_body(b, carry):
            total = unpair(conv_pairs(xd, b * per, per, big_2), per, cols).reshape(BLOCK, cols, chan)
            centre = xm[pl.ds(2 + b * BLOCK, BLOCK), :, chan : 2 * chan].astype(F32)
            total = total + centre
            ob[f, pl.ds(b * BLOCK, BLOCK)] = total.astype(BF16)
            if f + 1 < frames:
                for q in range(half):
                    to_blocks(f + 1, b, q, total[:, q * 2 * BLOCK : (q + 1) * 2 * BLOCK])
            return carry

        lax.fori_loop(0, band, last_body, 0)
        if f + 1 < frames:
            pack_and_send(f + 1)
        pltpu.make_async_copy(ob.at[f], out.at[f], out_sem.at[f]).start()

    for f in range(frames):
        pltpu.make_async_copy(ob.at[f], out.at[f], out_sem.at[f]).wait()
    each_side(lambda side: list_copy(side).wait_send())
    each_side(lambda side: feature_copy(side).wait_send())
    for f in range(frames):
        each_side(lambda side: pack_copy(f, side).wait_send())
        each_side(lambda side: halo_copy(f, side).wait_send())


def on_device(group, state, features, row_moves, col_moves, w_merge, w_first, w_second):
    frames, rows, cols, chan = features.shape
    band, across = rows // BLOCK, cols // BLOCK
    blocks = band * across
    slots = blocks // 2
    area = BLOCK * BLOCK
    me = lax.axis_index("rows")

    ids = jnp.arange(blocks, dtype=jnp.int32)
    src_row = jnp.clip(me * band + ids // across + row_moves, 0, band * group - 1)
    src_col = jnp.clip(ids % across + col_moves, 0, across - 1)
    rel = src_row - (me - 1) * band
    where_from = rel // band
    block = (rel % band) * across + src_col
    picks = block
    lists = []
    for side in (0, 1):
        mine = where_from == 2 * side
        earlier = mine[:, None, :] & (ids[None, None, :] < ids[None, :, None])
        rank = jnp.sum(earlier.astype(jnp.int32), axis=-1)
        hit = mine[:, None, :] & (rank[:, None, :] == jnp.arange(slots, dtype=jnp.int32)[None, :, None])
        lists.append(jnp.sum(jnp.where(hit, block[:, None, :], 0), axis=-1))
        picks = jnp.where(mine, blocks + side * slots + rank, picks)
    lists = jnp.pad(jnp.stack(lists), ((0, 0), (0, 8 - frames), (0, 128 - slots)))

    any_spec = pl.BlockSpec(memory_space=pl.ANY)
    copies = 2 + 2 * frames
    scratch = [
        pltpu.VMEM(state.shape, BF16),
        pltpu.VMEM(features.shape, BF16),
        pltpu.VMEM(w_merge.shape, BF16),
        pltpu.VMEM(w_first.shape, BF16),
        pltpu.VMEM(w_second.shape, BF16),
        [pltpu.VMEM((blocks, area, chan), BF16)] * frames,
        [pltpu.VMEM((blocks + 2 * slots, area, chan), BF16)] * frames,
        pltpu.VMEM((frames, 2, slots, area, chan), BF16),
        pltpu.VMEM((frames, rows + 6, cols, 3 * chan), BF16),
        pltpu.VMEM((rows + 6, cols, 3 * chan), BF16),
        pltpu.VMEM((rows + 4, cols, 3 * chan), BF16),
        pltpu.VMEM((rows + 2, cols, 3 * chan), BF16),
        pltpu.VMEM((frames, rows // 2 + 2, cols, 2 * chan), F32),
        pltpu.VMEM((frames, rows, cols, chan), BF16),
        pltpu.VMEM((frames, rows, cols, chan), BF16),
    ] + [pltpu.VMEM((12 * chan, 2 * chan), BF16)] * 4 + [
        pltpu.VMEM((2, 8, 128), jnp.int32),
        pltpu.SMEM((2, 8, 128), jnp.int32),
        pltpu.VMEM((2, frames, 3, cols, chan), BF16),
        pltpu.VMEM((frames, 2, 3, cols, chan), BF16),
        pltpu.SemaphoreType.DMA((5,)),
        pltpu.SemaphoreType.DMA((2,)),
        pltpu.SemaphoreType.DMA((frames,)),
        pltpu.SemaphoreType.DMA((copies, 2)),
        pltpu.SemaphoreType.DMA((copies, 2)),
    ]
    return pl.pallas_call(
        functools.partial(kernel, group),
        out_shape=jax.ShapeDtypeStruct(features.shape, BF16),
        in_specs=[
            pl.BlockSpec(memory_space=pltpu.SMEM),
            pl.BlockSpec(memory_space=pltpu.VMEM),
        ] + [any_spec] * 5,
        out_specs=any_spec,
        scratch_shapes=scratch,
        compiler_params=pltpu.CompilerParams(
            collective_id=0, has_side_effects=True, vmem_limit_bytes=58 * 1024 * 1024
        ),
    )(picks, lists, state, features, w_merge, w_first, w_second)


def solution(mesh):
    blocked = P(("clips", "rows"), None, None)
    framed = P(None, ("clips", "rows"), None, None)
    moves = P(None, ("clips", "rows"))
    return jax.shard_map(
        functools.partial(on_device, mesh.shape["rows"]),
        mesh=mesh,
        in_specs=(blocked, framed, moves, moves, P(), P(), P()),
        out_specs=framed,
        check_vma=False,
    )
```

```python
import functools

import jax
import jax.numpy as jnp
from jax import lax
from jax.experimental import pallas as pl
from jax.experimental.pallas import tpu as pltpu
from jax.sharding import PartitionSpec as P

BLOCK = 8
MESH = pl.DeviceIdType.MESH
F32 = jnp.float32
BF16 = jnp.bfloat16


def put_taps(dst, row, values, rows):
    cols, chan = dst.shape[1], dst.shape[2] // 3
    length = rows * cols
    col = lax.rem(lax.broadcasted_iota(jnp.int32, (length, chan), 0), cols)
    left = jnp.where(col == 0, 0.0, pltpu.roll(values, 1, 0))
    right = jnp.where(col == cols - 1, 0.0, pltpu.roll(values, length - 1, 0))
    for e, part in enumerate((left, values, right)):
        dst[pl.ds(row, rows), :, e * chan : (e + 1) * chan] = part.astype(BF16).reshape(rows, cols, chan)


def conv_pairs(src, pair, count, weight):
    cols, depth = src.shape[1], src.shape[2]
    rows = src[pl.ds(2 * pair, 2 * count + 2)].reshape(count + 1, 2, cols, depth)
    window = jnp.concatenate([rows[:count, 0], rows[:count, 1], rows[1:, 0], rows[1:, 1]], axis=-1)
    return jnp.dot(window.reshape(count * cols, 4 * depth), weight[...], preferred_element_type=F32)


def unpair(values, count, cols):
    chan = values.shape[1] // 2
    even = values[:, :chan].reshape(count, cols, chan)
    odd = values[:, chan:].reshape(count, cols, chan)
    return jnp.stack([even, odd], axis=1).reshape(2 * count * cols, chan)


def make_lists(me, group, band, across, row_moves, col_moves, moved, lists, picks_v):
    frames, blocks = row_moves.shape
    slots = lists.shape[1]
    lanes = moved.shape[2]
    moved[...] = jnp.zeros_like(moved)
    moved[0, :frames, :blocks] = row_moves[...]
    moved[1, :frames, :blocks] = col_moves[...]
    shape = moved.shape[1:]
    j = lax.broadcasted_iota(jnp.int32, shape, 1)
    src_row = jnp.clip(me * band + lax.div(j, across) + moved[0], 0, band * group - 1)
    src_col = jnp.clip(lax.rem(j, across) + moved[1], 0, across - 1)
    rel = src_row - (me - 1) * band
    valid = j < blocks
    within = jnp.where(rel < band, rel, jnp.where(rel < 2 * band, rel - band, rel - 2 * band))
    block = within * across + src_col
    picks = block
    slot = lax.broadcasted_iota(jnp.int32, (slots, lanes), 0)
    lane = lax.broadcasted_iota(jnp.int32, (slots, lanes), 1)
    for side in (0, 1):
        mine = valid & (rel < band if side == 0 else rel >= 2 * band)
        total = mine.astype(jnp.int32)
        step = 1
        while step < blocks:
            total = total + jnp.where(j >= step, pltpu.roll(total, step, 1), 0)
            step *= 2
        rank = jnp.where(mine, total - 1, -1)
        picks = jnp.where(mine, blocks + side * slots + rank, picks)
        wanted = jnp.zeros((slots, lanes), jnp.int32)
        for f in range(frames):
            hit = jnp.broadcast_to(rank[f : f + 1], (slots, lanes)) == slot
            column = jnp.sum(jnp.where(hit, jnp.broadcast_to(block[f : f + 1], (slots, lanes)), 0), axis=1, keepdims=True)
            wanted = jnp.where(lane == f, column, wanted)
        lists[side] = wanted
    picks_v[...] = picks


def kernel(
    group, row_moves, col_moves, state, features, w_merge, w_first, w_second, out,
    st, ft, wm, w1, w2, own, pool, packed, xf, xw, xm, xd, acc, wp,
    big_f, big_w, big_1, big_2, moved, lists, picks_v, picks, want_v, want, halo_f, halo_w,
    load_sem, want_sem, send_sem, recv_sem,
):
    frames, rows, cols, chan = features.shape
    band, across = rows // BLOCK, cols // BLOCK
    blocks = band * across
    slots = blocks // 2
    area = BLOCK * BLOCK
    me = lax.axis_index("rows")
    has = (me > 0, me < group - 1)
    peer = (me - 1, me + 1)

    loads = [
        pltpu.make_async_copy(a, b, load_sem.at[i])
        for i, (a, b) in enumerate(((state, st), (features, ft), (w_merge, wm), (w_first, w1), (w_second, w2)))
    ]
    for load in loads:
        load.start()

    barrier = pltpu.get_barrier_semaphore()
    for side in (0, 1):
        @pl.when(has[side])
        def _():
            pl.semaphore_signal(barrier, inc=1, device_id={"rows": peer[side]}, device_id_type=MESH)
    make_lists(me, group, band, across, row_moves, col_moves, moved, lists, picks_v)
    pl.semaphore_wait(barrier, has[0].astype(jnp.int32) + has[1].astype(jnp.int32))

    def remote(kind, side, src, dst):
        return pltpu.make_async_remote_copy(
            src_ref=src, dst_ref=dst,
            send_sem=send_sem.at[kind, side], recv_sem=recv_sem.at[kind, 1 - side],
            device_id={"rows": peer[side]}, device_id_type=MESH,
        )

    def list_copy(side):
        return remote(0, side, lists.at[side], want_v.at[1 - side])

    def feature_copy(f, side):
        edge = pl.ds(0, 3) if side == 0 else pl.ds(rows - 3, 3)
        return remote(1 + f, side, features.at[f, edge], halo_f.at[f, 1 - side])

    def pack_copy(f, side):
        return remote(1 + frames + f, side, packed.at[f, side], pool[f].at[pl.ds(blocks + (1 - side) * slots, slots)])

    def halo_copy(f, side):
        edge = pl.ds(0, 3) if side == 0 else pl.ds(rows - 3, 3)
        return remote(1 + 2 * frames + f, side, wp.at[f, edge], halo_w.at[f, 1 - side])

    def each_side(action):
        for side in (0, 1):
            @pl.when(has[side])
            def _():
                action(side)

    def arrived(copy_of, side):
        copy_of(1 - side).wait_recv()

    each_side(lambda side: list_copy(side).start())
    each_side(lambda side: feature_copy(0, side).start())
    picks_copy = pltpu.make_async_copy(picks_v, picks, want_sem.at[2])
    picks_copy.start()

    def to_blocks(f, b, q, strip):
        for h in (0, 1):
            block = strip[:, h * BLOCK : (h + 1) * BLOCK].reshape(area, chan).astype(BF16)
            own[f][b * across + 2 * q + h] = block
            pool[f][b * across + 2 * q + h] = block

    loads[0].wait()

    def cut_body(i, carry):
        b, q = i // (across // 2), i % (across // 2)
        strip = st[pl.ds(b * BLOCK, BLOCK), pl.ds(pl.multiple_of(q * 2 * BLOCK, 2 * BLOCK), 2 * BLOCK), :]
        to_blocks(0, b, q, strip.astype(F32))
        return carry

    lax.fori_loop(0, blocks // 2, cut_body, 0)

    for side in (0, 1):
        @pl.when(has[side])
        def _():
            arrived(list_copy, side)
            fetch = pltpu.make_async_copy(want_v.at[side], want.at[side], want_sem.at[side])
            fetch.start()
            fetch.wait()

    def pack_and_send(f):
        def action(side):
            def body(k, carry):
                for u in range(4):
                    packed[f, side, 4 * k + u] = own[f][want[side, 4 * k + u, f]]
                return carry
            lax.fori_loop(0, slots // 4, body, 0)
            pack_copy(f, side).start()
        each_side(action)

    pack_and_send(0)

    for load in loads[2:]:
        load.wait()

    def widen(big, raw, first):
        for t in range(4):
            for e in range(3):
                spot = pl.ds((t * 3 + e) * chan, chan)
                for r in (0, 1):
                    lanes = slice(r * chan, (r + 1) * chan)
                    if 0 <= t - r <= 2:
                        big[spot, lanes] = raw[t - r, e, first : first + chan, :]
                    else:
                        big[spot, lanes] = jnp.zeros((chan, chan), BF16)

    widen(big_f, wm, 0)
    widen(big_w, wm, chan)
    widen(big_1, w1, 0)
    widen(big_2, w2, 0)

    loads[1].wait()

    def fill_taps(dst, src, offset, total, step):
        def body(i, carry):
            values = src[pl.ds(i * step, step)].astype(F32).reshape(step * cols, chan)
            put_taps(dst, offset + i * step, values, step)
            return carry
        lax.fori_loop(0, total // step, body, 0)

    def edge_rows(dst, buffer, side):
        start = 0 if side == 0 else rows + 3
        values = buffer[...].astype(F32).reshape(3 * cols, chan)
        put_taps(dst, start, values, 3)

    def edge_zero(dst, start, count):
        dst[pl.ds(start, count)] = jnp.zeros((count,) + dst.shape[1:], BF16)

    pairs = rows // 2

    def feature_conv(f):
        fill_taps(xf, ft.at[f], 3, rows, 4)
        for side in (0, 1):
            @pl.when(has[side])
            def _():
                arrived(functools.partial(feature_copy, f), side)
                edge_rows(xf, halo_f.at[f, side], side)

        def feature_body(i, carry):
            count = (pairs + 2) // 3
            acc[pl.ds(i * count, count)] = conv_pairs(xf, i * count, count, big_f).reshape(count, cols, 2 * chan)
            return carry
        lax.fori_loop(0, 3, feature_body, 0)

    for side in (0, 1):
        @pl.when(jnp.logical_not(has[side]))
        def _():
            edge_zero(xf, 0 if side == 0 else rows + 3, 3)
            edge_zero(xw, 0 if side == 0 else rows + 3, 3)
    picks_copy.wait()

    def merge_pairs(f, pair, count):
        total = acc[pl.ds(pair, count)].reshape(count * cols, 2 * chan) + conv_pairs(xw, pair, count, big_w)
        total = jnp.maximum(total, 0.1 * total)
        put_taps(xm, 2 * pair, unpair(total, count, cols), 2 * count)

    for f in range(frames):
        feature_conv(f)
        each_side(lambda side: arrived(functools.partial(pack_copy, f), side))

        def gather_body(i, carry):
            b, q = i // (across // 2), i % (across // 2)
            halves = [
                pool[f][picks[f, b * across + 2 * q + h]].astype(F32).reshape(BLOCK, BLOCK, chan) for h in (0, 1)
            ]
            strip = jnp.concatenate(halves, axis=1).astype(BF16)
            wp[f, pl.ds(b * BLOCK, BLOCK), pl.ds(pl.multiple_of(q * 2 * BLOCK, 2 * BLOCK), 2 * BLOCK), :] = strip
            return carry

        half = across // 2
        lax.fori_loop(0, half, gather_body, 0)
        lax.fori_loop((band - 1) * half, band * half, gather_body, 0)
        each_side(lambda side: halo_copy(f, side).start())
        if f + 1 < frames:
            each_side(lambda side: feature_copy(f + 1, side).start())
        lax.fori_loop(half, (band - 1) * half, gather_body, 0)
        fill_taps(xw, wp.at[f], 3, rows, 4)

        inner = (pairs - 2) // 2
        lax.fori_loop(0, 2, lambda i, c: (merge_pairs(f, 2 + i * inner, inner), c)[1], 0)
        for side in (0, 1):
            @pl.when(has[side])
            def _():
                arrived(functools.partial(halo_copy, f), side)
                edge_rows(xw, halo_w.at[f, side], side)
            merge_pairs(f, 0 if side == 0 else pairs, 2)

            @pl.when(jnp.logical_not(has[side]))
            def _():
                edge_zero(xm, 0 if side == 0 else rows + 2, 2)

        count = (pairs + 1 + 2) // 3

        def middle_body(i, carry):
            pair = jnp.minimum(i * count, pairs + 1 - count)
            total = jnp.maximum(conv_pairs(xm, pair, count, big_1), 0.0)
            put_taps(xd, 2 * pair, unpair(total, count, cols), 2 * count)
            return carry

        lax.fori_loop(0, 3, middle_body, 0)
        for side in (0, 1):
            @pl.when(jnp.logical_not(has[side]))
            def _():
                edge_zero(xd, 0 if side == 0 else rows + 1, 1)

        per = BLOCK // 2

        def last_body(b, carry):
            total = unpair(conv_pairs(xd, b * per, per, big_2), per, cols).reshape(BLOCK, cols, chan)
            centre = xm[pl.ds(2 + b * BLOCK, BLOCK), :, chan : 2 * chan].astype(F32)
            total = total + centre
            out[f, pl.ds(b * BLOCK, BLOCK)] = total.astype(BF16)
            if f + 1 < frames:
                for q in range(half):
                    to_blocks(f + 1, b, q, total[:, q * 2 * BLOCK : (q + 1) * 2 * BLOCK])
            return carry

        lax.fori_loop(0, band, last_body, 0)
        if f + 1 < frames:
            pack_and_send(f + 1)

    each_side(lambda side: list_copy(side).wait_send())
    for f in range(frames):
        each_side(lambda side: feature_copy(f, side).wait_send())
        each_side(lambda side: pack_copy(f, side).wait_send())
        each_side(lambda side: halo_copy(f, side).wait_send())


def deliver(parts, held, out, sem):
    frames, rows = out.shape[:2]
    step = rows // parts
    copies = [
        pltpu.make_async_copy(held.at[f, pl.ds(i * step, step)], out.at[f, pl.ds(i * step, step)], sem.at[f, i])
        for f in range(frames)
        for i in range(parts)
    ]
    for copy in copies:
        copy.start()
    for copy in copies:
        copy.wait()


def on_device(group, state, features, row_moves, col_moves, w_merge, w_first, w_second):
    frames, rows, cols, chan = features.shape
    band, across = rows // BLOCK, cols // BLOCK
    blocks = band * across
    slots = blocks // 2
    area = BLOCK * BLOCK
    lanes = -(-blocks // 128) * 128
    any_spec = pl.BlockSpec(memory_space=pl.ANY)
    copies = 1 + 3 * frames
    scratch = [
        pltpu.VMEM(state.shape, BF16),
        pltpu.VMEM(features.shape, BF16),
        pltpu.VMEM(w_merge.shape, BF16),
        pltpu.VMEM(w_first.shape, BF16),
        pltpu.VMEM(w_second.shape, BF16),
        [pltpu.VMEM((blocks, area, chan), BF16)] * frames,
        [pltpu.VMEM((blocks + 2 * slots, area, chan), BF16)] * frames,
        pltpu.VMEM((frames, 2, slots, area, chan), BF16),
        pltpu.VMEM((rows + 6, cols, 3 * chan), BF16),
        pltpu.VMEM((rows + 6, cols, 3 * chan), BF16),
        pltpu.VMEM((rows + 4, cols, 3 * chan), BF16),
        pltpu.VMEM((rows + 2, cols, 3 * chan), BF16),
        pltpu.VMEM((rows // 2 + 2, cols, 2 * chan), F32),
        pltpu.VMEM((frames, rows, cols, chan), BF16),
    ] + [pltpu.VMEM((12 * chan, 2 * chan), BF16)] * 4 + [
        pltpu.VMEM((2, 8, lanes), jnp.int32),
        pltpu.VMEM((2, slots, lanes), jnp.int32),
        pltpu.VMEM((8, lanes), jnp.int32),
        pltpu.SMEM((8, lanes), jnp.int32),
        pltpu.VMEM((2, slots, lanes), jnp.int32),
        pltpu.SMEM((2, slots, lanes), jnp.int32),
        pltpu.VMEM((frames, 2, 3, cols, chan), BF16),
        pltpu.VMEM((frames, 2, 3, cols, chan), BF16),
        pltpu.SemaphoreType.DMA((5,)),
        pltpu.SemaphoreType.DMA((3,)),
        pltpu.SemaphoreType.DMA((copies, 2)),
        pltpu.SemaphoreType.DMA((copies, 2)),
    ]
    held = pl.pallas_call(
        functools.partial(kernel, group),
        out_shape=jax.ShapeDtypeStruct(features.shape, BF16),
        in_specs=[
            pl.BlockSpec(memory_space=pltpu.VMEM),
            pl.BlockSpec(memory_space=pltpu.VMEM),
        ] + [pl.BlockSpec(memory_space=pltpu.HBM)] * 5,
        out_specs=pl.BlockSpec(memory_space=pltpu.VMEM),
        scratch_shapes=scratch,
        compiler_params=pltpu.CompilerParams(
            collective_id=0, has_side_effects=True, vmem_limit_bytes=40 * 1024 * 1024
        ),
    )(row_moves, col_moves, state, features, w_merge, w_first, w_second)
    parts = 2
    return pl.pallas_call(
        functools.partial(deliver, parts),
        out_shape=jax.ShapeDtypeStruct(features.shape, BF16),
        in_specs=[any_spec],
        out_specs=any_spec,
        scratch_shapes=[pltpu.SemaphoreType.DMA((frames, parts))],
        compiler_params=pltpu.CompilerParams(vmem_limit_bytes=8 * 1024 * 1024),
    )(held)


def solution(mesh):
    blocked = P(("clips", "rows"), None, None)
    framed = P(None, ("clips", "rows"), None, None)
    moves = P(None, ("clips", "rows"))
    return jax.shard_map(
        functools.partial(on_device, mesh.shape["rows"]),
        mesh=mesh,
        in_specs=(blocked, framed, moves, moves, P(), P(), P()),
        out_specs=framed,
        check_vma=False,
    )
```
